512 devices in a mesh: player: 8 (over z), feat: 64 (over y, x, core).
Axes of the slice: x: 4, y: 8, z: 8, core: 2. Of those that a mesh axis runs over, the one named last changes fastest.
Arguments:
- slab: bfloat16 [128, 524288], P(None, 'feat'), may hold values from -16 to 16
- players: bfloat16 [512, 524288], P('player', 'feat'), may hold values from -16 to 16
Outputs:
- updated: bfloat16 [512, 524288], P('player', 'feat')
The draws below stay inside these ranges and needn't reach their ends.
All inputs are finite; a program needn't handle non-finite values.
Results may differ from the reference program's by a relative error of at most 0.0083.
Values may be sent and summed in bfloat16 or wider, within the bound.
A program may use at most 64 MiB of HBM per device.

```python
import math
import jax
import jax.numpy as jnp
from jax import lax

F = 524288
K = 512
B = 128
STEPS = 2


def slab_pair(key):
    base = jax.random.fold_in(key, 4242)
    key_slab = jax.random.fold_in(base, 0)
    key_mix = jax.random.fold_in(base, 1)
    key_noise = jax.random.fold_in(base, 2)
    key_freq = jax.random.fold_in(base, 5)
    key_phase = jax.random.fold_in(base, 6)
    unit_slab = jax.random.truncated_normal(key_slab, -4.0, 4.0, (B, F), jnp.float32)
    slab = jnp.clip(unit_slab, -16.0, 16.0)
    mixing = jax.random.normal(key_mix, (K, B), jnp.float32)
    span = 0.8 * jnp.dot(mixing, unit_slab) / math.sqrt(B)
    frequency = jax.random.uniform(key_freq, (K, 1), jnp.float32, 1.0, 3.0)
    phase = jax.random.uniform(key_phase, (K, 1), jnp.float32, 0.0, 1.0)
    position = jnp.arange(F, dtype=jnp.float32)[None, :] / F
    profile = 0.5 + 0.5 * jnp.sin(2.0 * math.pi * (frequency * position + phase))
    amplitude = jnp.exp(math.log(9.0) * (profile - 0.5))
    noise = 0.6 * jax.random.normal(key_noise, (K, F), jnp.float32) * amplitude
    players = jnp.clip(span + noise, -16.0, 16.0)
    return (slab, players)


def draw_slab(key, part):
    return slab_pair(key)[0].astype(jnp.bfloat16)


def draw_players(key, part):
    return slab_pair(key)[1].astype(jnp.bfloat16)


def setup_inputs(seed: int = 0) -> dict:
    splits = jax.random.split(jax.random.key(seed), 3)
    return {
        "slab": draw_slab(jax.random.fold_in(splits[2], 71), 0),
        "players": draw_players(jax.random.fold_in(splits[2], 71), 0),
    }


def reference(slab, players):
    block = min(64, K)
    count = K // block
    inverse_square = 1.0 / F / F
    weights = players
    rows = jnp.arange(K)[:, None]
    cols = jnp.arange(K)[None, :]
    for step in range(STEPS):
        proj = lax.dot_general(weights, slab, (((1,), (1,)), ((), ())), preferred_element_type=jnp.float32)
        scaled = (proj / F).astype(jnp.bfloat16)
        correlation = jnp.dot(proj, proj.T, precision=lax.Precision.HIGHEST) * inverse_square
        coeff = jnp.where(rows < cols, correlation, jnp.zeros_like(correlation)).astype(jnp.bfloat16)
        coeff_blocks = coeff.reshape(K, count, block).transpose(1, 0, 2)
        scaled_blocks = scaled.reshape(count, block, B)
        weight_blocks = weights.reshape(count, block, F)

        def one_block(items):
            own_rows, own_scaled, own_coeff = items
            reward = jnp.dot(own_scaled, slab, preferred_element_type=jnp.float32)
            penalty = lax.dot_general(own_coeff, weights, (((0,), (0,)), ((), ())), preferred_element_type=jnp.float32)
            update = own_rows.astype(jnp.float32) + reward - penalty
            total = lax.optimization_barrier(jnp.sum(update * update, axis=1))
            return (update * jnp.sqrt(F / (total + 1e-06))[:, None]).astype(jnp.bfloat16)
        weights = lax.map(one_block, (weight_blocks, scaled_blocks, coeff_blocks)).reshape(K, F)
    return weights
```

```python
import jax
import jax.numpy as jnp
from jax import lax
from jax.experimental import pallas as pl
from jax.experimental.pallas import tpu as pltpu
from jax.sharding import Mesh
from jax.sharding import PartitionSpec as P

F = 524288
EPS = 1e-06
K = 512
B = 128
OWN = 64
LOCAL = 8192
PIECE = 1024
CHUNK = 256
N = 8
AXES = ("player", "feat_0", "feat_1", "feat_2")
FEAT = AXES[1:]
MESH = pl.DeviceIdType.MESH
HIGHEST = lax.Precision.HIGHEST
F32 = jnp.float32
BF16 = jnp.bfloat16


def aligned(index, unit):
    return pl.multiple_of(index * unit, unit)


def exact_dot(a, b, dims):
    return lax.dot_general(a, b, (dims, ((), ())), precision=HIGHEST, preferred_element_type=F32)


def kernel(
    w_ref, x_ref, u_ref, scale_ref,
    wv, xv, wcat, partial, from_y, reduced, from_xc, by_z, to_y, by_y, pg, a1, m2, c2, u1, u1b, base, u2b,
    n1_a, n1_b, n1_c, n2_a, n2_b, n2_c, columns,
    load_sem, send_sem, recv_sem,
):
    z = lax.axis_index("player")
    y = lax.axis_index("feat_0")
    x = lax.axis_index("feat_1")
    c = lax.axis_index("feat_2")

    def along_z(d):
        return {"player": lax.rem(z + d, N)}

    def along_y(d):
        return {"feat_0": lax.rem(y + d, N)}

    def along_xc(d):
        return {"feat_1": lax.rem(x + d // 2, 4), "feat_2": lax.rem(c + d % 2, 2)}

    def send(src, dst, stage, device):
        pltpu.make_async_remote_copy(
            src_ref=src,
            dst_ref=dst,
            send_sem=send_sem.at[stage],
            recv_sem=recv_sem.at[stage],
            device_id=device,
            device_id_type=MESH,
        ).start()

    def wait_recv(view, stage):
        pltpu.make_async_copy(view, view, recv_sem.at[stage]).wait()

    def wait_send(view, stage):
        pltpu.make_async_copy(view, view, send_sem.at[stage]).wait()

    load_x = pltpu.make_async_copy(x_ref, xv, load_sem.at[0])
    load_w = pltpu.make_async_copy(w_ref, wv, load_sem.at[1])
    own_cols = pl.ds(aligned(z, PIECE), PIECE)
    own_rows = pl.ds(aligned(z, OWN), OWN)
    load_own = pltpu.make_async_copy(w_ref.at[:, own_cols], wcat.at[own_rows, :], load_sem.at[2])
    load_slab = pltpu.make_async_copy(x_ref.at[:, own_cols], wcat.at[pl.ds(K, B), :], load_sem.at[3])
    barrier = pltpu.get_barrier_semaphore()
    for route in (along_z, along_y, along_xc):
        for d in range(1, N):
            pl.semaphore_signal(barrier, inc=1, device_id=route(d), device_id_type=MESH)
    load_w.start()
    load_x.start()
    load_own.start()
    load_slab.start()
    pl.semaphore_wait(barrier, 3 * (N - 1))

    for d in (1, 7, 2, 6, 3, 5, 4):
        peer = lax.rem(z + d, N)
        send(w_ref.at[:, pl.ds(aligned(peer, PIECE), PIECE)], wcat.at[own_rows, :], 0, along_z(d))

    load_w.wait()
    load_x.wait()
    rows = (((1,), (1,)), ((), ()))
    own_proj = lax.dot_general(wv[...], xv[...], rows, preferred_element_type=F32)
    own_gram = lax.dot_general(xv[...], xv[...], rows, preferred_element_type=F32)
    for i in range(N):
        partial[i, 0:8] = own_proj[8 * i : 8 * i + 8]
        partial[i, 8:24] = own_gram[16 * i : 16 * i + 16]
    for d in range(1, N):
        send(partial.at[lax.rem(y + d, N)], from_y.at[d], 1, along_y(d))
    wait_recv(from_y.at[pl.ds(1, N - 1)], 1)
    total = partial[y]
    for d in range(1, N):
        total += from_y[d]
    reduced[...] = total
    for d in range(1, N):
        send(reduced, from_xc.at[d], 2, along_xc(d))
    wait_recv(from_xc.at[pl.ds(1, N - 1)], 2)
    for d in range(1, N):
        total += from_xc[d]
    by_z[z] = total[0:8]
    for d in range(1, N):
        send(by_z.at[z], by_z.at[z], 3, along_z(d))
    to_y[64:80] = total[8:24]
    wait_recv(by_z.at[pl.ds(1, N - 1)], 3)
    for i in range(N):
        to_y[8 * i : 8 * i + 8] = by_z[i]
    by_y[y] = to_y[...]
    for d in range(1, N):
        send(to_y, by_y.at[y], 4, along_y(d))
    wait_recv(by_y.at[pl.ds(1, N - 1)], 4)
    for i in range(N):
        for j in range(N):
            pg[64 * i + 8 * j : 64 * i + 8 * j + 8] = by_y[j, 8 * i : 8 * i + 8]
        pg[K + 16 * i : K + 16 * i + 16] = by_y[i, 64:80]

    earlier = lax.broadcasted_iota(jnp.int32, (K, K), 1) < lax.broadcasted_iota(jnp.int32, (K, K), 0)
    inverse_square = 1.0 / F / F
    proj = pg[0:K]
    corr = exact_dot(proj, proj, ((1,), (1,))) * inverse_square
    a1[:, 0:K] = jnp.where(earlier, -corr, 0.0).astype(BF16)
    a1[:, K : K + B] = (proj * (1.0 / F)).astype(BF16)
    proj2 = proj + exact_dot(a1[...].astype(F32), pg[...], ((1,), (0,)))
    corr2 = exact_dot(proj2, proj2, ((1,), (1,))) * inverse_square
    m2[...] = jnp.where(earlier, -corr2, 0.0)
    q2 = (proj2 * (1.0 / F)).astype(BF16)

    load_own.wait()
    load_slab.wait()
    wait_recv(wcat.at[pl.ds(0, K - OWN)], 0)

    def squares_of(value):
        wide = value * value
        return sum(wide[:, B * i : B * i + B] for i in range(CHUNK // B))

    def as_row(squares):
        return jnp.sum(jnp.transpose(squares), axis=0, keepdims=True)

    def first(i, squares):
        cols = pl.ds(aligned(i, CHUNK), CHUNK)
        value = wcat[0:K, cols].astype(F32) + jnp.dot(a1[...], wcat[:, cols], preferred_element_type=F32)
        u1[:, cols] = value
        u1b[:, cols] = value.astype(BF16)
        return squares + squares_of(value)

    squares = lax.fori_loop(0, PIECE // CHUNK, first, jnp.zeros((K, B), F32))

    def all_sum(value, bufs, stage):
        for buf, route, s in zip(bufs, (along_xc, along_y, along_z), range(stage, stage + 3)):
            buf[0] = value
            for d in range(1, N):
                send(buf.at[0], buf.at[d], s, route(d))
            if s == stage:
                yield None
            wait_recv(buf.at[pl.ds(1, N - 1)], s)
            for d in range(1, N):
                value += buf[d]
        yield value

    summing = all_sum(as_row(squares), (n1_a, n1_b, n1_c), 5)
    next(summing)

    def second_base(i, carry):
        cols = pl.ds(aligned(i, CHUNK), CHUNK)
        base[:, cols] = u1[:, cols] + jnp.dot(q2, wcat[K : K + B, cols], preferred_element_type=F32)
        return carry

    lax.fori_loop(0, PIECE // CHUNK, second_base, 0)
    n1 = next(summing)
    c2[...] = (m2[...] * (F / (n1 + EPS))).astype(BF16)

    def second(lo, hi):
        def body(i, squares):
            cols = pl.ds(aligned(i, CHUNK), CHUNK)
            value = base[lo:hi, cols] + jnp.dot(
                c2[lo:hi, 0:hi], u1b[0:hi, cols], preferred_element_type=F32
            )
            u2b[lo:hi, cols] = value.astype(BF16)
            return squares + squares_of(value)

        return lax.fori_loop(0, PIECE // CHUNK, body, jnp.zeros((hi - lo, B), F32))

    halves = [second(0, K // 2), second(K // 2, K)]
    summing = all_sum(as_row(jnp.concatenate(halves, axis=0)), (n2_a, n2_b, n2_c), 9)
    for d in (1, 7, 2, 6, 3, 5, 4):
        peer = lax.rem(z + d, N)
        send(u2b.at[pl.ds(aligned(peer, OWN), OWN), :], u_ref.at[:, own_cols], 8, along_z(d))
    keep = pltpu.make_async_copy(u2b.at[own_rows, :], u_ref.at[:, own_cols], load_sem.at[4])
    keep.start()
    next(summing)
    n2 = next(summing)
    scale = jnp.sqrt(F / (n2 + EPS * (n1 + EPS) / F))
    columns[...] = jnp.transpose(jnp.broadcast_to(scale, (B, K)))
    scale_ref[...] = columns[own_rows, :]

    wait_send(wcat.at[pl.ds(0, K - OWN)], 0)
    wait_send(from_y.at[pl.ds(1, N - 1)], 1)
    wait_send(from_xc.at[pl.ds(1, N - 1)], 2)
    wait_send(by_z.at[pl.ds(1, N - 1)], 3)
    wait_send(by_y.at[pl.ds(1, N - 1)], 4)
    for buf, stage in ((n1_a, 5), (n1_b, 6), (n1_c, 7), (n2_a, 9), (n2_b, 10), (n2_c, 11)):
        wait_send(buf.at[pl.ds(1, N - 1)], stage)
    keep.wait()
    wait_recv(u2b.at[pl.ds(0, K - OWN)], 8)
    wait_send(u2b.at[pl.ds(0, K - OWN)], 8)


def on_device(slab, players):
    def vmem(*shape, dtype=F32):
        return pltpu.VMEM(shape, dtype)

    update, scale = pl.pallas_call(
        kernel,
        out_shape=[
            jax.ShapeDtypeStruct((OWN, LOCAL), BF16),
            jax.ShapeDtypeStruct((OWN, B), F32),
        ],
        in_specs=[pl.BlockSpec(memory_space=pl.ANY)] * 2,
        out_specs=[
            pl.BlockSpec(memory_space=pl.ANY),
            pl.BlockSpec(memory_space=pltpu.VMEM),
        ],
        scratch_shapes=[
            vmem(OWN, LOCAL, dtype=BF16),
            vmem(B, LOCAL, dtype=BF16),
            vmem(K + B, PIECE, dtype=BF16),
            vmem(N, 24, B),
            vmem(N, 24, B),
            vmem(24, B),
            vmem(N, 24, B),
            vmem(N, 8, B),
            vmem(80, B),
            vmem(N, 80, B),
            vmem(K + B, B),
            vmem(K, K + B, dtype=BF16),
            vmem(K, K),
            vmem(K, K, dtype=BF16),
            vmem(K, PIECE),
            vmem(K, PIECE, dtype=BF16),
            vmem(K, PIECE),
            vmem(K, PIECE, dtype=BF16),
            *[vmem(N, 1, K) for _ in range(6)],
            vmem(K, B),
            pltpu.SemaphoreType.DMA((5,)),
            pltpu.SemaphoreType.DMA((12,)),
            pltpu.SemaphoreType.DMA((12,)),
        ],
        compiler_params=pltpu.CompilerParams(
            collective_id=0, has_side_effects=True, vmem_limit_bytes=48 * 1024 * 1024
        ),
    )(players, slab)
    return (update.astype(F32) * scale[:, 0:1]).astype(BF16)


def solution(mesh):
    split = Mesh(mesh.devices.reshape(N, 8, 4, 2), AXES)
    in_specs = (P(None, FEAT), P("player", FEAT))
    out_specs = P("player", FEAT)
    return jax.shard_map(on_device, mesh=split, in_specs=in_specs, out_specs=out_specs, check_vma=False)
```

```python
import jax
import jax.numpy as jnp
from jax import lax
from jax.experimental import pallas as pl
from jax.experimental.pallas import tpu as pltpu
from jax.sharding import Mesh
from jax.sharding import PartitionSpec as P

F = 524288
EPS = 1e-06
K = 512
B = 128
OWN = 64
LOCAL = 8192
PIECE = 1024
CHUNK = 256
N = 8
AXES = ("player", "feat_0", "feat_1", "feat_2")
FEAT = AXES[1:]
MESH = pl.DeviceIdType.MESH
HALF = K // 2
NEAR = (1, 7, 3, 5)
FAR = (2, 6, 4)
F32 = jnp.float32
BF16 = jnp.bfloat16


def aligned(index, unit):
    return pl.multiple_of(index * unit, unit)


def halves_of(value):
    high = value.astype(BF16)
    return high, (value - high.astype(F32)).astype(BF16)


def lower_products(value, out, offset, scale, dtype):
    high, low = halves_of(value)
    left = jnp.concatenate([high, high, low], axis=1)
    right = jnp.concatenate([high, low, high], axis=1)
    for first in (0, HALF):
        size = first + HALF
        corr = lax.dot_general(
            left[first:size], right[0:size], (((1,), (1,)), ((), ())), preferred_element_type=F32
        )
        row = first + lax.broadcasted_iota(jnp.int32, corr.shape, 0)
        earlier = lax.broadcasted_iota(jnp.int32, corr.shape, 1) < row
        out[first:size, offset : offset + size] = jnp.where(earlier, corr * scale, 0.0).astype(dtype)


def kernel(
    w_ref, x_ref, u_ref, scale_ref,
    wv, xv, wcat, proj_part, proj_xc, proj_y, by_z, by_xc, gram_part, gram_xc, gram_y, gram, pg, a1, m2, c2, u1, u1b, base, u2b,
    n1_a, n1_b, n2_a, n2_b, columns,
    load_sem, send_sem, recv_sem,
):
    z = lax.axis_index("player")
    y = lax.axis_index("feat_0")
    x = lax.axis_index("feat_1")
    c = lax.axis_index("feat_2")

    def along_z(d):
        return {"player": lax.rem(z + d, N)}

    def along_y(d):
        return {"feat_0": lax.rem(y + d, N)}

    def along_xc(d):
        return {"feat_1": lax.rem(x + d // 2, 4), "feat_2": lax.rem(c + d % 2, 2)}

    def along_zc(d):
        return {"player": lax.rem(z + d // 2, N), "feat_2": lax.rem(c + d % 2, 2)}

    def along_yx(d):
        return {"feat_0": lax.rem(y + d // 4, N), "feat_1": lax.rem(x + d % 4, 4)}

    def send(src, dst, stage, device):
        pltpu.make_async_remote_copy(
            src_ref=src,
            dst_ref=dst,
            send_sem=send_sem.at[stage],
            recv_sem=recv_sem.at[stage],
            device_id=device,
            device_id_type=MESH,
        ).start()

    def wait_recv(view, stage):
        pltpu.make_async_copy(view, view, recv_sem.at[stage]).wait()

    def wait_send(view, stage):
        pltpu.make_async_copy(view, view, send_sem.at[stage]).wait()

    own_cols = pl.ds(aligned(z, PIECE), PIECE)
    own_rows = pl.ds(aligned(z, OWN), OWN)
    own_in_cat = pl.ds(aligned(z, OWN) + B, OWN)
    load_w = pltpu.make_async_copy(w_ref, wv, load_sem.at[0])
    load_x = pltpu.make_async_copy(x_ref, xv, load_sem.at[1])
    load_own = pltpu.make_async_copy(w_ref.at[:, own_cols], wcat.at[own_in_cat, :], load_sem.at[2])
    load_slab = pltpu.make_async_copy(x_ref.at[:, own_cols], wcat.at[pl.ds(0, B), :], load_sem.at[3])
    load_w.start()
    load_x.start()
    load_own.start()
    load_slab.start()
    barrier = pltpu.get_barrier_semaphore()
    for route, offsets in ((along_zc, range(1, 16)), (along_yx, range(1, 32)), (along_xc, (3, 5, 7))):
        for d in offsets:
            pl.semaphore_signal(barrier, inc=1, device_id=route(d), device_id_type=MESH)
    pl.semaphore_wait(barrier, 49)

    def send_players(offsets):
        for d in offsets:
            peer = lax.rem(z + d, N)
            send(w_ref.at[:, pl.ds(aligned(peer, PIECE), PIECE)], wcat.at[own_in_cat, :], 0, along_z(d))

    send_players(NEAR)

    own = 2 * x + c

    def piece_of(d):
        return 2 * lax.rem(x + d // 2, 4) + lax.rem(c + d % 2, 2)

    def rows_times_slab(value):
        return lax.dot_general(value, xv[...], (((1,), (1,)), ((), ())), preferred_element_type=F32)

    def added(first, buf):
        for d in range(1, N):
            first += buf[d]
        return first

    load_w.wait()
    load_x.wait()
    proj_part[...] = rows_times_slab(wv[...]).reshape(N, 8, B)
    for d in range(1, N):
        send(proj_part.at[piece_of(d)], proj_xc.at[d], 1, along_xc(d))
    gram_part[...] = rows_times_slab(xv[...]).reshape(N, 16, B)
    for d in range(1, N):
        send(gram_part.at[piece_of(d)], gram_xc.at[d], 2, along_xc(d))
    wait_recv(proj_xc.at[pl.ds(1, N - 1)], 1)
    proj_y[0] = added(proj_part[own], proj_xc)
    for d in range(1, N):
        send(proj_y.at[0], proj_y.at[d], 3, along_y(d))
    wait_recv(gram_xc.at[pl.ds(1, N - 1)], 2)
    gram_y[0] = added(gram_part[own], gram_xc)
    for d in range(1, N):
        send(gram_y.at[0], gram_y.at[d], 4, along_y(d))
    wait_recv(proj_y.at[pl.ds(1, N - 1)], 3)
    by_z[z] = added(proj_y[0], proj_y)
    for d in range(1, N):
        send(by_z.at[z], by_z.at[z], 5, along_z(d))
    send_players(FAR)
    wait_recv(gram_y.at[pl.ds(1, N - 1)], 4)
    gram[own] = added(gram_y[0], gram_y)
    for d in range(1, N):
        send(gram.at[own], gram.at[own], 6, along_xc(d))
    wait_recv(by_z.at[pl.ds(1, N - 1)], 5)
    by_xc[own] = by_z[...]
    for d in range(1, N):
        send(by_z, by_xc.at[own], 7, along_xc(d))
    wait_recv(by_xc.at[pl.ds(1, N - 1)], 7)
    for i in range(N):
        for j in range(N):
            pg[B + 64 * i + 8 * j : B + 64 * i + 8 * j + 8] = by_xc[j, i]

    inverse_square = 1.0 / F / F
    proj = pg[B : B + K]
    lower_products(proj, a1, B, -inverse_square, BF16)
    a1[:, 0:B] = (proj * (1.0 / F)).astype(BF16)

    load_own.wait()
    load_slab.wait()
    wait_recv(wcat.at[pl.ds(0, K - OWN)], 0)

    def squares_of(value):
        wide = value * value
        return sum(wide[:, B * i : B * i + B] for i in range(CHUNK // B))

    def as_row(squares):
        return jnp.sum(jnp.transpose(squares), axis=0, keepdims=True)

    squares = []
    for first in (0, HALF):
        size = first + HALF

        def body(i, total, first=first, size=size):
            cols = pl.ds(aligned(i, CHUNK), CHUNK)
            value = wcat[B + first : B + size, cols].astype(F32) + jnp.dot(
                a1[first:size, 0 : B + size], wcat[0 : B + size, cols], preferred_element_type=F32
            )
            u1[first:size, cols] = value
            u1b[first:size, cols] = value.astype(BF16)
            return total + squares_of(value)

        squares.append(lax.fori_loop(0, PIECE // CHUNK, body, jnp.zeros((HALF, B), F32), unroll=2))

    def all_sum(value, bufs, stage):
        for buf, route, s in zip(bufs, (along_zc, along_yx), (stage, stage + 1)):
            count = buf.shape[0]
            buf[0] = value
            for d in range(1, count):
                send(buf.at[0], buf.at[d], s, route(d))
            yield None
            wait_recv(buf.at[pl.ds(1, count - 1)], s)
            for d in range(1, count):
                value += buf[d]
        yield value

    summing = all_sum(as_row(jnp.concatenate(squares, axis=0)), (n1_a, n1_b), 8)
    next(summing)

    wait_recv(gram.at[pl.ds(1, N - 1)], 6)
    for i in range(N):
        pg[16 * i : 16 * i + 16] = gram[i]
    high, low = halves_of(pg[...])
    split = jnp.concatenate([high, low], axis=1)
    proj2 = []
    for first in (0, HALF):
        size = first + HALF
        terms = jnp.dot(a1[first:size, 0 : B + size], split[0 : B + size], preferred_element_type=F32)
        proj2.append(proj[first:size] + terms[:, 0:B] + terms[:, B : 2 * B])
    proj2 = jnp.concatenate(proj2, axis=0)
    lower_products(proj2, m2, 0, -inverse_square, F32)
    q2 = (proj2 * (1.0 / F)).astype(BF16)
    next(summing)

    def second_base(i, carry):
        cols = pl.ds(aligned(i, CHUNK), CHUNK)
        base[:, cols] = u1[:, cols] + jnp.dot(q2, wcat[0:B, cols], preferred_element_type=F32)
        return carry

    lax.fori_loop(0, PIECE // CHUNK, second_base, 0)
    n1 = next(summing)
    spread = F / (n1 + EPS)

    squares = []
    for first in (0, HALF):
        size = first + HALF
        c2[first:size, 0:size] = (m2[first:size, 0:size] * spread[:, 0:size]).astype(BF16)

        def body(i, total, first=first, size=size):
            cols = pl.ds(aligned(i, CHUNK), CHUNK)
            value = base[first:size, cols] + jnp.dot(
                c2[first:size, 0:size], u1b[0:size, cols], preferred_element_type=F32
            )
            u2b[first:size, cols] = value.astype(BF16)
            return total + squares_of(value)

        squares.append(lax.fori_loop(0, PIECE // CHUNK, body, jnp.zeros((HALF, B), F32), unroll=2))
    summing = all_sum(as_row(jnp.concatenate(squares, axis=0)), (n2_a, n2_b), 11)
    next(summing)
    for d in (1, 7, 2, 6, 3, 5, 4):
        peer = lax.rem(z + d, N)
        send(u2b.at[pl.ds(aligned(peer, OWN), OWN), :], u_ref.at[:, own_cols], 10, along_z(d))
    keep = pltpu.make_async_copy(u2b.at[own_rows, :], u_ref.at[:, own_cols], load_sem.at[4])
    keep.start()
    next(summing)
    n2 = next(summing)
    scale = jnp.sqrt(F / (n2 + EPS * (n1 + EPS) / F))
    columns[...] = jnp.transpose(jnp.broadcast_to(scale, (B, K)))
    scale_ref[...] = columns[own_rows, :]

    wait_send(wcat.at[pl.ds(0, K - OWN)], 0)
    for buf, stage in (
        (proj_xc, 1), (gram_xc, 2), (proj_y, 3), (gram_y, 4), (by_z, 5), (gram, 6), (by_xc, 7),
        (n1_a, 8), (n1_b, 9), (n2_a, 11), (n2_b, 12),
    ):
        wait_send(buf.at[pl.ds(1, buf.shape[0] - 1)], stage)
    keep.wait()
    wait_recv(u2b.at[pl.ds(0, K - OWN)], 10)
    wait_send(u2b.at[pl.ds(0, K - OWN)], 10)


def on_device(slab, players):
    def vmem(*shape, dtype=F32):
        return pltpu.VMEM(shape, dtype)

    update, scale = pl.pallas_call(
        kernel,
        out_shape=[
            jax.ShapeDtypeStruct((OWN, LOCAL), BF16),
            jax.ShapeDtypeStruct((OWN, B), F32),
        ],
        in_specs=[pl.BlockSpec(memory_space=pltpu.HBM)] * 2,
        out_specs=[
            pl.BlockSpec(memory_space=pl.ANY),
            pl.BlockSpec(memory_space=pltpu.VMEM),
        ],
        scratch_shapes=[
            vmem(OWN, LOCAL, dtype=BF16),
            vmem(B, LOCAL, dtype=BF16),
            vmem(B + K, PIECE, dtype=BF16),
            vmem(N, 8, B),
            vmem(N, 8, B),
            vmem(N, 8, B),
            vmem(N, 8, B),
            vmem(N, N, 8, B),
            vmem(N, 16, B),
            vmem(N, 16, B),
            vmem(N, 16, B),
            vmem(N, 16, B),
            vmem(B + K, B),
            vmem(K, B + K, dtype=BF16),
            vmem(K, K),
            vmem(K, K, dtype=BF16),
            vmem(K, PIECE),
            vmem(K, PIECE, dtype=BF16),
            vmem(K, PIECE),
            vmem(K, PIECE, dtype=BF16),
            vmem(16, 1, K),
            vmem(32, 1, K),
            vmem(16, 1, K),
            vmem(32, 1, K),
            vmem(K, B),
            pltpu.SemaphoreType.DMA((5,)),
            pltpu.SemaphoreType.DMA((13,)),
            pltpu.SemaphoreType.DMA((13,)),
        ],
        compiler_params=pltpu.CompilerParams(
            collective_id=0, has_side_effects=True, vmem_limit_bytes=48 * 1024 * 1024
        ),
    )(players, slab)
    return (update.astype(F32) * scale[:, 0:1]).astype(BF16)


def solution(mesh):
    split = Mesh(mesh.devices.reshape(N, 8, 4, 2), AXES)
    in_specs = (P(None, FEAT), P("player", FEAT))
    out_specs = P("player", FEAT)
    return jax.shard_map(on_device, mesh=split, in_specs=in_specs, out_specs=out_specs, check_vma=False)
```

```python
import jax
import jax.numpy as jnp
from jax import lax
from jax.experimental import pallas as pl
from jax.experimental.pallas import tpu as pltpu
from jax.sharding import Mesh
from jax.sharding import PartitionSpec as P

F = 524288
EPS = 1e-06
K = 512
B = 128
OWN = 64
LOCAL = 8192
PIECE = 1024
CHUNK = 256
EARLY = 768
N = 8
AXES = ("player", "feat_0", "feat_1", "feat_2")
FEAT = AXES[1:]
MESH = pl.DeviceIdType.MESH
HALF = K // 2
NEAR = (1, 7, 3, 5)
FAR = (2, 6, 4)
F32 = jnp.float32
BF16 = jnp.bfloat16


def aligned(index, unit):
    return pl.multiple_of(index * unit, unit)


def halves_of(value):
    high = value.astype(BF16)
    return high, (value - high.astype(F32)).astype(BF16)


def lower_products(value, out, offset, scale, dtype):
    high, low = halves_of(value)
    left = jnp.concatenate([high, high, low], axis=1)
    right = jnp.concatenate([high, low, high], axis=1)
    for first in (0, HALF):
        size = first + HALF
        corr = lax.dot_general(
            left[first:size], right[0:size], (((1,), (1,)), ((), ())), preferred_element_type=F32
        )
        row = first + lax.broadcasted_iota(jnp.int32, corr.shape, 0)
        earlier = lax.broadcasted_iota(jnp.int32, corr.shape, 1) < row
        out[first:size, offset : offset + size] = jnp.where(earlier, corr * scale, 0.0).astype(dtype)


def kernel(
    w_ref, x_ref, u_ref, scale_ref,
    wv, xv, wcat, proj_part, proj_xc, proj_y, by_z, by_xc, gram_part, gram_xc, gram_y, gram, pg, a1, m2, c2, u1, u1b, base, u2b,
    n1_a, n1_b, n2_a, n2_b, columns,
    load_sem, send_sem, recv_sem,
):
    z = lax.axis_index("player")
    y = lax.axis_index("feat_0")
    x = lax.axis_index("feat_1")
    c = lax.axis_index("feat_2")

    def along_z(d):
        return {"player": lax.rem(z + d, N)}

    def along_y(d):
        return {"feat_0": lax.rem(y + d, N)}

    def along_xc(d):
        return {"feat_1": lax.rem(x + d // 2, 4), "feat_2": lax.rem(c + d % 2, 2)}

    def along_zc(d):
        return {"player": lax.rem(z + d // 2, N), "feat_2": lax.rem(c + d % 2, 2)}

    def along_yx(d):
        return {"feat_0": lax.rem(y + d // 4, N), "feat_1": lax.rem(x + d % 4, 4)}

    def send(src, dst, stage, device):
        pltpu.make_async_remote_copy(
            src_ref=src,
            dst_ref=dst,
            send_sem=send_sem.at[stage],
            recv_sem=recv_sem.at[stage],
            device_id=device,
            device_id_type=MESH,
        ).start()

    def wait_recv(view, stage):
        pltpu.make_async_copy(view, view, recv_sem.at[stage]).wait()

    def wait_send(view, stage):
        pltpu.make_async_copy(view, view, send_sem.at[stage]).wait()

    own_cols = pl.ds(aligned(z, PIECE), PIECE)
    own_rows = pl.ds(aligned(z, OWN), OWN)
    own_in_cat = pl.ds(aligned(z, OWN) + B, OWN)
    load_w = pltpu.make_async_copy(w_ref, wv, load_sem.at[0])
    load_x = pltpu.make_async_copy(x_ref, xv, load_sem.at[1])
    load_own = pltpu.make_async_copy(w_ref.at[:, own_cols], wcat.at[own_in_cat, :], load_sem.at[2])
    load_slab = pltpu.make_async_copy(x_ref.at[:, own_cols], wcat.at[pl.ds(0, B), :], load_sem.at[3])
    load_w.start()
    load_x.start()
    load_own.start()
    load_slab.start()
    barrier = pltpu.get_barrier_semaphore()
    for route, offsets in ((along_zc, range(1, 16)), (along_yx, range(1, 32)), (along_xc, (3, 5, 7))):
        for d in offsets:
            pl.semaphore_signal(barrier, inc=1, device_id=route(d), device_id_type=MESH)
    pl.semaphore_wait(barrier, 49)

    def send_players(offsets, begin, width, stage):
        for d in offsets:
            peer = lax.rem(z + d, N)
            send(
                w_ref.at[:, pl.ds(aligned(peer, PIECE) + begin, width)],
                wcat.at[own_in_cat, pl.ds(begin, width)],
                stage,
                along_z(d),
            )

    send_players(NEAR, 0, PIECE, 0)

    own = 2 * x + c

    def piece_of(d):
        return 2 * lax.rem(x + d // 2, 4) + lax.rem(c + d % 2, 2)

    def rows_times_slab(value):
        return lax.dot_general(value, xv[...], (((1,), (1,)), ((), ())), preferred_element_type=F32)

    def added(first, buf):
        for d in range(1, N):
            first += buf[d]
        return first

    load_w.wait()
    load_x.wait()
    proj_part[...] = rows_times_slab(wv[...]).reshape(N, 8, B)
    for d in range(1, N):
        send(proj_part.at[piece_of(d)], proj_xc.at[d], 1, along_xc(d))
    gram_part[...] = rows_times_slab(xv[...]).reshape(N, 16, B)
    for d in range(1, N):
        send(gram_part.at[piece_of(d)], gram_xc.at[d], 2, along_xc(d))
    wait_recv(proj_xc.at[pl.ds(1, N - 1)], 1)
    proj_y[0] = added(proj_part[own], proj_xc)
    for d in range(1, N):
        send(proj_y.at[0], proj_y.at[d], 3, along_y(d))
    wait_recv(gram_xc.at[pl.ds(1, N - 1)], 2)
    gram_y[0] = added(gram_part[own], gram_xc)
    for d in range(1, N):
        send(gram_y.at[0], gram_y.at[d], 4, along_y(d))
    wait_recv(proj_y.at[pl.ds(1, N - 1)], 3)
    by_z[z] = added(proj_y[0], proj_y)
    for d in range(1, N):
        send(by_z.at[z], by_z.at[z], 5, along_z(d))
    send_players(FAR, 0, EARLY, 14)
    send_players(FAR, EARLY, PIECE - EARLY, 15)
    wait_recv(gram_y.at[pl.ds(1, N - 1)], 4)
    gram[own] = added(gram_y[0], gram_y)
    for d in range(1, N):
        send(gram.at[own], gram.at[own], 6, along_xc(d))
    wait_recv(by_z.at[pl.ds(1, N - 1)], 5)
    by_xc[own] = by_z[...]
    for d in range(1, N):
        send(by_z, by_xc.at[own], 7, along_xc(d))
    wait_recv(by_xc.at[pl.ds(1, N - 1)], 7)
    for i in range(N):
        for j in range(N):
            pg[B + 64 * i + 8 * j : B + 64 * i + 8 * j + 8] = by_xc[j, i]

    inverse_square = 1.0 / F / F
    proj = pg[B : B + K]
    lower_products(proj, a1, B, -inverse_square, BF16)
    a1[:, 0:B] = (proj * (1.0 / F)).astype(BF16)

    load_own.wait()
    load_slab.wait()

    def squares_of(value):
        wide = value * value
        return sum(wide[:, B * i : B * i + B] for i in range(CHUNK // B))

    def as_row(squares):
        return jnp.sum(jnp.transpose(squares), axis=0, keepdims=True)

    near = wcat.at[pl.ds(0, OWN * len(NEAR))]
    early = wcat.at[pl.ds(0, OWN * len(FAR)), pl.ds(0, EARLY)]
    late = wcat.at[pl.ds(0, OWN * len(FAR)), pl.ds(EARLY, PIECE - EARLY)]

    def first_update(i, totals):
        cols = pl.ds(aligned(i, CHUNK), CHUNK)
        out = []
        for first, total in zip((0, HALF), totals):
            size = first + HALF
            value = wcat[B + first : B + size, cols].astype(F32) + jnp.dot(
                a1[first:size, 0 : B + size], wcat[0 : B + size, cols], preferred_element_type=F32
            )
            u1[first:size, cols] = value
            u1b[first:size, cols] = value.astype(BF16)
            out.append(total + squares_of(value))
        return tuple(out)

    wait_recv(near, 0)
    wait_recv(early, 14)
    squares = (jnp.zeros((HALF, B), F32),) * 2
    squares = lax.fori_loop(0, EARLY // CHUNK, first_update, squares, unroll=True)
    wait_recv(late, 15)
    squares = lax.fori_loop(EARLY // CHUNK, PIECE // CHUNK, first_update, squares, unroll=True)

    def hops(d, inner):
        far, near = d // inner, d % inner
        return min(far, N - far) + min(near, inner - near)

    def all_sum(value, bufs, stage):
        for buf, route, inner, s in zip(bufs, (along_zc, along_yx), (2, 4), (stage, stage + 1)):
            count = buf.shape[0]
            buf[0] = value
            for d in sorted(range(1, count), key=lambda d: -hops(d, inner)):
                send(buf.at[0], buf.at[d], s, route(d))
            yield None
            wait_recv(buf.at[pl.ds(1, count - 1)], s)
            for d in range(1, count):
                value += buf[d]
        yield value

    summing = all_sum(as_row(jnp.concatenate(squares, axis=0)), (n1_a, n1_b), 8)
    next(summing)

    wait_recv(gram.at[pl.ds(1, N - 1)], 6)
    for i in range(N):
        pg[16 * i : 16 * i + 16] = gram[i]
    high, low = halves_of(pg[...])
    split = jnp.concatenate([high, low], axis=1)
    proj2 = []
    for first in (0, HALF):
        size = first + HALF
        terms = jnp.dot(a1[first:size, 0 : B + size], split[0 : B + size], preferred_element_type=F32)
        proj2.append(proj[first:size] + terms[:, 0:B] + terms[:, B : 2 * B])
    proj2 = jnp.concatenate(proj2, axis=0)
    lower_products(proj2, m2, 0, -inverse_square, F32)
    q2 = (proj2 * (1.0 / F)).astype(BF16)
    next(summing)

    def second_base(i, carry):
        cols = pl.ds(aligned(i, CHUNK), CHUNK)
        base[:, cols] = u1[:, cols] + jnp.dot(q2, wcat[0:B, cols], preferred_element_type=F32)
        return carry

    lax.fori_loop(0, PIECE // CHUNK, second_base, 0)
    n1 = next(summing)
    spread = F / (n1 + EPS)

    for first in (0, HALF):
        size = first + HALF
        c2[first:size, 0:size] = (m2[first:size, 0:size] * spread[:, 0:size]).astype(BF16)

    def second(i, totals):
        cols = pl.ds(aligned(i, CHUNK), CHUNK)
        out = []
        for first, total in zip((0, HALF), totals):
            size = first + HALF
            value = base[first:size, cols] + jnp.dot(
                c2[first:size, 0:size], u1b[0:size, cols], preferred_element_type=F32
            )
            u2b[first:size, cols] = value.astype(BF16)
            out.append(total + squares_of(value))
        return tuple(out)

    def send_updates(begin, width, stage):
        for d in (1, 7, 2, 6, 3, 5, 4):
            peer = lax.rem(z + d, N)
            send(
                u2b.at[pl.ds(aligned(peer, OWN), OWN), pl.ds(begin, width)],
                u_ref.at[:, pl.ds(aligned(z, PIECE) + begin, width)],
                stage,
                along_z(d),
            )

    squares = second(0, (jnp.zeros((HALF, B), F32),) * 2)
    send_updates(0, CHUNK, 10)
    squares = lax.fori_loop(1, PIECE // CHUNK, second, squares, unroll=True)
    summing = all_sum(as_row(jnp.concatenate(squares, axis=0)), (n2_a, n2_b), 11)
    next(summing)
    send_updates(CHUNK, PIECE - CHUNK, 13)
    keep = pltpu.make_async_copy(u2b.at[own_rows, :], u_ref.at[:, own_cols], load_sem.at[4])
    keep.start()
    next(summing)
    n2 = next(summing)
    scale = jnp.sqrt(F / (n2 + EPS * (n1 + EPS) / F))
    columns[...] = jnp.transpose(jnp.broadcast_to(scale, (B, K)))
    scale_ref[...] = columns[own_rows, :]

    wait_send(near, 0)
    wait_send(early, 14)
    wait_send(late, 15)
    for buf, stage in (
        (proj_xc, 1), (gram_xc, 2), (proj_y, 3), (gram_y, 4), (by_z, 5), (gram, 6), (by_xc, 7),
        (n1_a, 8), (n1_b, 9), (n2_a, 11), (n2_b, 12),
    ):
        wait_send(buf.at[pl.ds(1, buf.shape[0] - 1)], stage)
    keep.wait()
    for begin, width, stage in ((0, CHUNK, 10), (CHUNK, PIECE - CHUNK, 13)):
        sent = u2b.at[pl.ds(0, K - OWN), pl.ds(begin, width)]
        wait_recv(sent, stage)
        wait_send(sent, stage)


def on_device(slab, players):
    def vmem(*shape, dtype=F32):
        return pltpu.VMEM(shape, dtype)

    update, scale = pl.pallas_call(
        kernel,
        out_shape=[
            jax.ShapeDtypeStruct((OWN, LOCAL), BF16),
            jax.ShapeDtypeStruct((OWN, B), F32),
        ],
        in_specs=[pl.BlockSpec(memory_space=pltpu.HBM)] * 2,
        out_specs=[
            pl.BlockSpec(memory_space=pl.ANY),
            pl.BlockSpec(memory_space=pltpu.VMEM),
        ],
        scratch_shapes=[
            vmem(OWN, LOCAL, dtype=BF16),
            vmem(B, LOCAL, dtype=BF16),
            vmem(B + K, PIECE, dtype=BF16),
            vmem(N, 8, B),
            vmem(N, 8, B),
            vmem(N, 8, B),
            vmem(N, 8, B),
            vmem(N, N, 8, B),
            vmem(N, 16, B),
            vmem(N, 16, B),
            vmem(N, 16, B),
            vmem(N, 16, B),
            vmem(B + K, B),
            vmem(K, B + K, dtype=BF16),
            vmem(K, K),
            vmem(K, K, dtype=BF16),
            vmem(K, PIECE),
            vmem(K, PIECE, dtype=BF16),
            vmem(K, PIECE),
            vmem(K, PIECE, dtype=BF16),
            vmem(16, 1, K),
            vmem(32, 1, K),
            vmem(16, 1, K),
            vmem(32, 1, K),
            vmem(K, B),
            pltpu.SemaphoreType.DMA((5,)),
            pltpu.SemaphoreType.DMA((16,)),
            pltpu.SemaphoreType.DMA((16,)),
        ],
        compiler_params=pltpu.CompilerParams(
            collective_id=0, has_side_effects=True, vmem_limit_bytes=60 * 1024 * 1024
        ),
    )(players, slab)
    return (update.astype(F32) * scale[:, 0:1]).astype(BF16)


def solution(mesh):
    split = Mesh(mesh.devices.reshape(N, 8, 4, 2), AXES)
    in_specs = (P(None, FEAT), P("player", FEAT))
    out_specs = P("player", FEAT)
    return jax.shard_map(on_device, mesh=split, in_specs=in_specs, out_specs=out_specs, check_vma=False)
```

```python
import jax
import jax.numpy as jnp
from jax import lax
from jax.experimental import pallas as pl
from jax.experimental.pallas import tpu as pltpu
from jax.sharding import Mesh
from jax.sharding import PartitionSpec as P

F = 524288
EPS = 1e-06
K = 512
B = 128
OWN = 64
LOCAL = 8192
PIECE = 1024
CHUNK = 256
EARLY = 768
N = 8
AXES = ("player", "feat_0", "feat_1", "feat_2")
FEAT = AXES[1:]
MESH = pl.DeviceIdType.MESH
HALF = K // 2
NEAR = (4, 2, 6)
FAR = (3, 5, 1, 7)
F32 = jnp.float32
BF16 = jnp.bfloat16


def aligned(index, unit):
    return pl.multiple_of(index * unit, unit)


def halves_of(value):
    high = value.astype(BF16)
    return high, (value - high.astype(F32)).astype(BF16)


def lower_products(value, out, offset, scale, dtype):
    high, low = halves_of(value)
    left = jnp.concatenate([high, high, low], axis=1)
    right = jnp.concatenate([high, low, high], axis=1)
    for first in (0, HALF):
        size = first + HALF
        corr = lax.dot_general(
            left[first:size], right[0:size], (((1,), (1,)), ((), ())), preferred_element_type=F32
        )
        row = first + lax.broadcasted_iota(jnp.int32, corr.shape, 0)
        earlier = lax.broadcasted_iota(jnp.int32, corr.shape, 1) < row
        out[first:size, offset : offset + size] = jnp.where(earlier, corr * scale, 0.0).astype(dtype)


def kernel(
    w_ref, x_ref, u_ref, scale_ref,
    wv, xv, wcat, proj_part, proj_xc, proj_y, by_z, by_xc, gram_part, gram_xc, gram_y, gram, pg, a1, m2, c2, u1, u1b, base, u2b,
    n1_a, n1_b, n2_a, n2_b, columns,
    load_sem, send_sem, recv_sem,
):
    z = lax.axis_index("player")
    y = lax.axis_index("feat_0")
    x = lax.axis_index("feat_1")
    c = lax.axis_index("feat_2")

    def along_z(d):
        return {"player": lax.rem(z + d, N)}

    def along_y(d):
        return {"feat_0": lax.rem(y + d, N)}

    def along_xc(d):
        return {"feat_1": lax.rem(x + d // 2, 4), "feat_2": lax.rem(c + d % 2, 2)}

    def along_zc(d):
        return {"player": lax.rem(z + d // 2, N), "feat_2": lax.rem(c + d % 2, 2)}

    def along_yx(d):
        return {"feat_0": lax.rem(y + d // 4, N), "feat_1": lax.rem(x + d % 4, 4)}

    def send(src, dst, stage, device):
        pltpu.make_async_remote_copy(
            src_ref=src,
            dst_ref=dst,
            send_sem=send_sem.at[stage],
            recv_sem=recv_sem.at[stage],
            device_id=device,
            device_id_type=MESH,
        ).start()

    def wait_recv(view, stage):
        pltpu.make_async_copy(view, view, recv_sem.at[stage]).wait()

    def wait_send(view, stage):
        pltpu.make_async_copy(view, view, send_sem.at[stage]).wait()

    own_cols = pl.ds(aligned(z, PIECE), PIECE)
    own_rows = pl.ds(aligned(z, OWN), OWN)
    own_in_cat = pl.ds(aligned(z, OWN) + B, OWN)
    load_w = pltpu.make_async_copy(w_ref, wv, load_sem.at[0])
    load_x = pltpu.make_async_copy(x_ref, xv, load_sem.at[1])
    load_own = pltpu.make_async_copy(w_ref.at[:, own_cols], wcat.at[own_in_cat, :], load_sem.at[2])
    load_slab = pltpu.make_async_copy(x_ref.at[:, own_cols], wcat.at[pl.ds(0, B), :], load_sem.at[3])
    load_w.start()
    load_x.start()
    load_own.start()
    load_slab.start()
    barrier = pltpu.get_barrier_semaphore()
    for route, offsets in ((along_zc, range(1, 16)), (along_yx, range(1, 32)), (along_xc, (3, 5, 7))):
        for d in offsets:
            pl.semaphore_signal(barrier, inc=1, device_id=route(d), device_id_type=MESH)
    pl.semaphore_wait(barrier, 49)

    def send_players(offsets, begin, width, stage):
        for d in offsets:
            peer = lax.rem(z + d, N)
            send(
                w_ref.at[:, pl.ds(aligned(peer, PIECE) + begin, width)],
                wcat.at[own_in_cat, pl.ds(begin, width)],
                stage,
                along_z(d),
            )

    send_players(NEAR, 0, PIECE, 0)

    own = 2 * x + c

    def piece_of(d):
        return 2 * lax.rem(x + d // 2, 4) + lax.rem(c + d % 2, 2)

    def rows_times_slab(value):
        return lax.dot_general(value, xv[...], (((1,), (1,)), ((), ())), preferred_element_type=F32)

    def added(first, buf):
        for d in range(1, N):
            first += buf[d]
        return first

    load_w.wait()
    load_x.wait()
    proj_part[...] = rows_times_slab(wv[...]).reshape(N, 8, B)
    for d in range(1, N):
        send(proj_part.at[piece_of(d)], proj_xc.at[d], 1, along_xc(d))
    gram_part[...] = rows_times_slab(xv[...]).reshape(N, 16, B)
    for d in range(1, N):
        send(gram_part.at[piece_of(d)], gram_xc.at[d], 2, along_xc(d))
    wait_recv(proj_xc.at[pl.ds(1, N - 1)], 1)
    proj_y[0] = added(proj_part[own], proj_xc)
    for d in range(1, N):
        send(proj_y.at[0], proj_y.at[d], 3, along_y(d))
    wait_recv(gram_xc.at[pl.ds(1, N - 1)], 2)
    gram_y[0] = added(gram_part[own], gram_xc)
    for d in range(1, N):
        send(gram_y.at[0], gram_y.at[d], 4, along_y(d))
    wait_recv(proj_y.at[pl.ds(1, N - 1)], 3)
    by_z[z] = added(proj_y[0], proj_y)
    for d in range(1, N):
        send(by_z.at[z], by_z.at[z], 5, along_z(d))
    send_players(FAR, 0, EARLY, 14)
    send_players(FAR, EARLY, PIECE - EARLY, 15)
    wait_recv(gram_y.at[pl.ds(1, N - 1)], 4)
    gram[own] = added(gram_y[0], gram_y)
    for d in range(1, N):
        send(gram.at[own], gram.at[own], 6, along_xc(d))
    wait_recv(by_z.at[pl.ds(1, N - 1)], 5)
    by_xc[own] = by_z[...]
    for d in range(1, N):
        send(by_z, by_xc.at[own], 7, along_xc(d))
    wait_recv(by_xc.at[pl.ds(1, N - 1)], 7)
    for i in range(N):
        for j in range(N):
            pg[B + 64 * i + 8 * j : B + 64 * i + 8 * j + 8] = by_xc[j, i]

    inverse_square = 1.0 / F / F
    proj = pg[B : B + K]
    lower_products(proj, a1, B, -inverse_square, BF16)
    a1[:, 0:B] = (proj * (1.0 / F)).astype(BF16)

    load_own.wait()
    load_slab.wait()

    def squares_of(value):
        wide = value * value
        return sum(wide[:, B * i : B * i + B] for i in range(CHUNK // B))

    def as_row(squares):
        return jnp.sum(jnp.transpose(squares), axis=0, keepdims=True)

    near = wcat.at[pl.ds(0, OWN * len(NEAR))]
    early = wcat.at[pl.ds(0, OWN * len(FAR)), pl.ds(0, EARLY)]
    late = wcat.at[pl.ds(0, OWN * len(FAR)), pl.ds(EARLY, PIECE - EARLY)]

    def first_update(i, totals):
        cols = pl.ds(aligned(i, CHUNK), CHUNK)
        out = []
        for first, total in zip((0, HALF), totals):
            size = first + HALF
            value = wcat[B + first : B + size, cols].astype(F32) + jnp.dot(
                a1[first:size, 0 : B + size], wcat[0 : B + size, cols], preferred_element_type=F32
            )
            u1[first:size, cols] = value
            u1b[first:size, cols] = value.astype(BF16)
            out.append(total + squares_of(value))
        return tuple(out)

    wait_recv(near, 0)
    wait_recv(early, 14)
    squares = (jnp.zeros((HALF, B), F32),) * 2
    squares = lax.fori_loop(0, EARLY // CHUNK, first_update, squares, unroll=True)
    wait_recv(late, 15)
    squares = lax.fori_loop(EARLY // CHUNK, PIECE // CHUNK, first_update, squares, unroll=True)

    def hops(d, inner):
        far, near = d // inner, d % inner
        return min(far, N - far) + min(near, inner - near)

    def all_sum(value, bufs, stage):
        for buf, route, inner, s in zip(bufs, (along_zc, along_yx), (2, 4), (stage, stage + 1)):
            count = buf.shape[0]
            buf[0] = value
            for d in sorted(range(1, count), key=lambda d: -hops(d, inner)):
                send(buf.at[0], buf.at[d], s, route(d))
            yield None
            wait_recv(buf.at[pl.ds(1, count - 1)], s)
            for d in range(1, count):
                value += buf[d]
        yield value

    summing = all_sum(as_row(jnp.concatenate(squares, axis=0)), (n1_a, n1_b), 8)
    next(summing)

    wait_recv(gram.at[pl.ds(1, N - 1)], 6)
    for i in range(N):
        pg[16 * i : 16 * i + 16] = gram[i]
    high, low = halves_of(pg[...])
    split = jnp.concatenate([high, low], axis=1)
    proj2 = []
    for first in (0, HALF):
        size = first + HALF
        terms = jnp.dot(a1[first:size, 0 : B + size], split[0 : B + size], preferred_element_type=F32)
        proj2.append(proj[first:size] + terms[:, 0:B] + terms[:, B : 2 * B])
    proj2 = jnp.concatenate(proj2, axis=0)
    lower_products(proj2, m2, 0, -inverse_square, F32)
    q2 = (proj2 * (1.0 / F)).astype(BF16)
    next(summing)

    def second_base(i, carry):
        cols = pl.ds(aligned(i, CHUNK), CHUNK)
        base[:, cols] = u1[:, cols] + jnp.dot(q2, wcat[0:B, cols], preferred_element_type=F32)
        return carry

    lax.fori_loop(0, PIECE // CHUNK, second_base, 0)
    n1 = next(summing)
    spread = F / (n1 + EPS)

    for first in (0, HALF):
        size = first + HALF
        c2[first:size, 0:size] = (m2[first:size, 0:size] * spread[:, 0:size]).astype(BF16)

    def second(i, totals):
        cols = pl.ds(aligned(i, CHUNK), CHUNK)
        out = []
        for first, total in zip((0, HALF), totals):
            size = first + HALF
            value = base[first:size, cols] + jnp.dot(
                c2[first:size, 0:size], u1b[0:size, cols], preferred_element_type=F32
            )
            u2b[first:size, cols] = value.astype(BF16)
            out.append(total + squares_of(value))
        return tuple(out)

    def send_updates(begin, width, stage):
        for d in (1, 7, 2, 6, 3, 5, 4):
            peer = lax.rem(z + d, N)
            send(
                u2b.at[pl.ds(aligned(peer, OWN), OWN), pl.ds(begin, width)],
                u_ref.at[:, pl.ds(aligned(z, PIECE) + begin, width)],
                stage,
                along_z(d),
            )

    squares = second(0, (jnp.zeros((HALF, B), F32),) * 2)
    send_updates(0, CHUNK, 10)
    squares = lax.fori_loop(1, PIECE // CHUNK, second, squares, unroll=True)
    summing = all_sum(as_row(jnp.concatenate(squares, axis=0)), (n2_a, n2_b), 11)
    next(summing)
    send_updates(CHUNK, PIECE - CHUNK, 13)
    keep = pltpu.make_async_copy(u2b.at[own_rows, :], u_ref.at[:, own_cols], load_sem.at[4])
    keep.start()
    next(summing)
    n2 = next(summing)
    scale = jnp.sqrt(F / (n2 + EPS * (n1 + EPS) / F))
    columns[...] = jnp.transpose(jnp.broadcast_to(scale, (B, K)))
    scale_ref[...] = columns[own_rows, :]

    wait_send(near, 0)
    wait_send(early, 14)
    wait_send(late, 15)
    for buf, stage in (
        (proj_xc, 1), (gram_xc, 2), (proj_y, 3), (gram_y, 4), (by_z, 5), (gram, 6), (by_xc, 7),
        (n1_a, 8), (n1_b, 9), (n2_a, 11), (n2_b, 12),
    ):
        wait_send(buf.at[pl.ds(1, buf.shape[0] - 1)], stage)
    keep.wait()
    for begin, width, stage in ((0, CHUNK, 10), (CHUNK, PIECE - CHUNK, 13)):
        sent = u2b.at[pl.ds(0, K - OWN), pl.ds(begin, width)]
        wait_recv(sent, stage)
        wait_send(sent, stage)


def on_device(slab, players):
    def vmem(*shape, dtype=F32):
        return pltpu.VMEM(shape, dtype)

    update, scale = pl.pallas_call(
        kernel,
        out_shape=[
            jax.ShapeDtypeStruct((OWN, LOCAL), BF16),
            jax.ShapeDtypeStruct((OWN, B), F32),
        ],
        in_specs=[pl.BlockSpec(memory_space=pltpu.HBM)] * 2,
        out_specs=[
            pl.BlockSpec(memory_space=pl.ANY),
            pl.BlockSpec(memory_space=pltpu.VMEM),
        ],
        scratch_shapes=[
            vmem(OWN, LOCAL, dtype=BF16),
            vmem(B, LOCAL, dtype=BF16),
            vmem(B + K, PIECE, dtype=BF16),
            vmem(N, 8, B),
            vmem(N, 8, B),
            vmem(N, 8, B),
            vmem(N, 8, B),
            vmem(N, N, 8, B),
            vmem(N, 16, B),
            vmem(N, 16, B),
            vmem(N, 16, B),
            vmem(N, 16, B),
            vmem(B + K, B),
            vmem(K, B + K, dtype=BF16),
            vmem(K, K),
            vmem(K, K, dtype=BF16),
            vmem(K, PIECE),
            vmem(K, PIECE, dtype=BF16),
            vmem(K, PIECE),
            vmem(K, PIECE, dtype=BF16),
            vmem(16, 1, K),
            vmem(32, 1, K),
            vmem(16, 1, K),
            vmem(32, 1, K),
            vmem(K, B),
            pltpu.SemaphoreType.DMA((5,)),
            pltpu.SemaphoreType.DMA((16,)),
            pltpu.SemaphoreType.DMA((16,)),
        ],
        compiler_params=pltpu.CompilerParams(
            collective_id=0, has_side_effects=True, vmem_limit_bytes=52 * 1024 * 1024
        ),
    )(players, slab)
    return (update.astype(F32) * scale[:, 0:1]).astype(BF16)


def solution(mesh):
    split = Mesh(mesh.devices.reshape(N, 8, 4, 2), AXES)
    in_specs = (P(None, FEAT), P("player", FEAT))
    out_specs = P("player", FEAT)
    return jax.shard_map(on_device, mesh=split, in_specs=in_specs, out_specs=out_specs, check_vma=False)
```

```python
import jax
import jax.numpy as jnp
from jax import lax
from jax.experimental import pallas as pl
from jax.experimental.pallas import tpu as pltpu
from jax.sharding import Mesh
from jax.sharding import PartitionSpec as P

F = 524288
EPS = 1e-06
K = 512
B = 128
OWN = 64
LOCAL = 8192
PIECE = 1024
CHUNK = 256
EARLY = 768
N = 8
AXES = ("player", "feat_0", "feat_1", "feat_2")
FEAT = AXES[1:]
MESH = pl.DeviceIdType.MESH
HALF = K // 2
NEAR = (4, 2, 6)
FAR = (3, 5, 1, 7)
F32 = jnp.float32
BF16 = jnp.bfloat16


def aligned(index, unit):
    return pl.multiple_of(index * unit, unit)


def halves_of(value):
    high = value.astype(BF16)
    return high, (value - high.astype(F32)).astype(BF16)


def lower_products(value, out, offset, scale, dtype):
    high, low = halves_of(value)
    left = jnp.concatenate([high, high, low], axis=1)
    right = jnp.concatenate([high, low, high], axis=1)
    for first in (0, HALF):
        size = first + HALF
        corr = lax.dot_general(
            left[first:size], right[0:size], (((1,), (1,)), ((), ())), preferred_element_type=F32
        )
        row = first + lax.broadcasted_iota(jnp.int32, corr.shape, 0)
        earlier = lax.broadcasted_iota(jnp.int32, corr.shape, 1) < row
        out[first:size, offset : offset + size] = jnp.where(earlier, corr * scale, 0.0).astype(dtype)


def kernel(
    w_ref, x_ref, u_ref, scale_ref,
    wv, xv, wcat, proj_part, proj_xc, proj_y, by_z, by_xc, gram_part, gram_xc, gram_y, gram, pg, a1, m2, c2, u1, u1b, base, u2b,
    n1_a, n1_b, n2_a, n2_b, columns,
    load_sem, send_sem, recv_sem,
):
    z = lax.axis_index("player")
    y = lax.axis_index("feat_0")
    x = lax.axis_index("feat_1")
    c = lax.axis_index("feat_2")

    def along_z(d):
        return {"player": lax.rem(z + d, N)}

    def along_y(d):
        return {"feat_0": lax.rem(y + d, N)}

    def along_xc(d):
        return {"feat_1": lax.rem(x + d // 2, 4), "feat_2": lax.rem(c + d % 2, 2)}

    def along_zc(d):
        return {"player": lax.rem(z + d // 2, N), "feat_2": lax.rem(c + d % 2, 2)}

    def along_yx(d):
        return {"feat_0": lax.rem(y + d // 4, N), "feat_1": lax.rem(x + d % 4, 4)}

    def send(src, dst, stage, device):
        pltpu.make_async_remote_copy(
            src_ref=src,
            dst_ref=dst,
            send_sem=send_sem.at[stage],
            recv_sem=recv_sem.at[stage],
            device_id=device,
            device_id_type=MESH,
        ).start()

    def wait_recv(view, stage):
        pltpu.make_async_copy(view, view, recv_sem.at[stage]).wait()

    def wait_send(view, stage):
        pltpu.make_async_copy(view, view, send_sem.at[stage]).wait()

    own_cols = pl.ds(aligned(z, PIECE), PIECE)
    own_rows = pl.ds(aligned(z, OWN), OWN)
    own_in_cat = pl.ds(aligned(z, OWN) + B, OWN)
    load_w = pltpu.make_async_copy(w_ref, wv, load_sem.at[0])
    load_x = pltpu.make_async_copy(x_ref, xv, load_sem.at[1])
    load_own = pltpu.make_async_copy(w_ref.at[:, own_cols], wcat.at[own_in_cat, :], load_sem.at[2])
    load_slab = pltpu.make_async_copy(x_ref.at[:, own_cols], wcat.at[pl.ds(0, B), :], load_sem.at[3])
    load_w.start()
    load_x.start()
    load_own.start()
    load_slab.start()
    barrier = pltpu.get_barrier_semaphore()
    for route, offsets in ((along_zc, range(1, 16)), (along_yx, range(1, 32)), (along_xc, (3, 5, 7))):
        for d in offsets:
            pl.semaphore_signal(barrier, inc=1, device_id=route(d), device_id_type=MESH)
    pl.semaphore_wait(barrier, 49)

    def send_players(offsets, begin, width, stage):
        for d in offsets:
            peer = lax.rem(z + d, N)
            send(
                w_ref.at[:, pl.ds(aligned(peer, PIECE) + begin, width)],
                wcat.at[own_in_cat, pl.ds(begin, width)],
                stage,
                along_z(d),
            )

    send_players(NEAR, 0, PIECE, 0)

    own = 2 * x + c

    def piece_of(d):
        return 2 * lax.rem(x + d // 2, 4) + lax.rem(c + d % 2, 2)

    def rows_times_slab(value):
        return lax.dot_general(value, xv[...], (((1,), (1,)), ((), ())), preferred_element_type=F32)

    def added(first, buf):
        for d in range(1, N):
            first += buf[d]
        return first

    load_w.wait()
    load_x.wait()
    proj_part[...] = rows_times_slab(wv[...]).reshape(N, 8, B)
    for d in range(1, N):
        send(proj_part.at[piece_of(d)], proj_xc.at[d], 1, along_xc(d))
    gram_part[...] = rows_times_slab(xv[...]).reshape(N, 16, B)
    for d in range(1, N):
        send(gram_part.at[piece_of(d)], gram_xc.at[d], 2, along_xc(d))
    wait_recv(proj_xc.at[pl.ds(1, N - 1)], 1)
    proj_y[0] = added(proj_part[own], proj_xc)
    for d in range(1, N):
        send(proj_y.at[0], proj_y.at[d], 3, along_y(d))
    wait_recv(gram_xc.at[pl.ds(1, N - 1)], 2)
    gram_y[0] = added(gram_part[own], gram_xc)
    for d in range(1, N):
        send(gram_y.at[0], gram_y.at[d], 4, along_y(d))
    wait_recv(proj_y.at[pl.ds(1, N - 1)], 3)
    by_z[z] = added(proj_y[0], proj_y)
    for d in range(1, N):
        send(by_z.at[z], by_z.at[z], 5, along_z(d))
    send_players(FAR, 0, EARLY, 14)
    send_players(FAR, EARLY, PIECE - EARLY, 15)
    wait_recv(gram_y.at[pl.ds(1, N - 1)], 4)
    gram[own] = added(gram_y[0], gram_y)
    for d in range(1, N):
        send(gram.at[own], gram.at[own], 6, along_xc(d))
    wait_recv(by_z.at[pl.ds(1, N - 1)], 5)
    by_xc[own] = by_z[...]
    for d in range(1, N):
        send(by_z, by_xc.at[own], 7, along_xc(d))
    wait_recv(by_xc.at[pl.ds(1, N - 1)], 7)
    for i in range(N):
        for j in range(N):
            pg[B + 64 * i + 8 * j : B + 64 * i + 8 * j + 8] = by_xc[j, i]

    inverse_square = 1.0 / F / F
    proj = pg[B : B + K]
    lower_products(proj, a1, B, -inverse_square, BF16)
    a1[:, 0:B] = (proj * (1.0 / F)).astype(BF16)

    load_own.wait()
    load_slab.wait()

    def squares_of(value):
        wide = value * value
        return sum(wide[:, B * i : B * i + B] for i in range(CHUNK // B))

    def as_row(squares):
        return jnp.sum(jnp.transpose(squares), axis=0, keepdims=True)

    near = wcat.at[pl.ds(0, OWN * len(NEAR))]
    early = wcat.at[pl.ds(0, OWN * len(FAR)), pl.ds(0, EARLY)]
    late = wcat.at[pl.ds(0, OWN * len(FAR)), pl.ds(EARLY, PIECE - EARLY)]

    def first_update(i, totals):
        cols = pl.ds(aligned(i, CHUNK), CHUNK)
        out = []
        for first, total in zip((0, HALF), totals):
            size = first + HALF
            value = wcat[B + first : B + size, cols].astype(F32) + jnp.dot(
                a1[first:size, 0 : B + size], wcat[0 : B + size, cols], preferred_element_type=F32
            )
            u1[first:size, cols] = value
            u1b[first:size, cols] = value.astype(BF16)
            out.append(total + squares_of(value))
        return tuple(out)

    wait_recv(near, 0)
    wait_recv(early, 14)
    squares = (jnp.zeros((HALF, B), F32),) * 2
    squares = lax.fori_loop(0, EARLY // CHUNK, first_update, squares, unroll=True)
    wait_recv(late, 15)
    squares = lax.fori_loop(EARLY // CHUNK, PIECE // CHUNK, first_update, squares, unroll=True)

    def hops(d, inner):
        far, near = d // inner, d % inner
        return min(far, N - far) + min(near, inner - near)

    def all_sum(value, bufs, stage):
        for buf, route, inner, s in zip(bufs, (along_zc, along_yx), (2, 4), (stage, stage + 1)):
            count = buf.shape[0]
            buf[0] = value
            for d in sorted(range(1, count), key=lambda d: -hops(d, inner)):
                send(buf.at[0], buf.at[d], s, route(d))
            yield None
            wait_recv(buf.at[pl.ds(1, count - 1)], s)
            for d in range(1, count):
                value += buf[d]
        yield value

    summing = all_sum(as_row(jnp.concatenate(squares, axis=0)), (n1_a, n1_b), 8)
    next(summing)

    wait_recv(gram.at[pl.ds(1, N - 1)], 6)
    for i in range(N):
        pg[16 * i : 16 * i + 16] = gram[i]
    high, low = halves_of(pg[...])
    split = jnp.concatenate([high, low], axis=1)
    proj2 = []
    for first in (0, HALF):
        size = first + HALF
        terms = jnp.dot(a1[first:size, 0 : B + size], split[0 : B + size], preferred_element_type=F32)
        proj2.append(proj[first:size] + terms[:, 0:B] + terms[:, B : 2 * B])
    proj2 = jnp.concatenate(proj2, axis=0)
    lower_products(proj2, m2, 0, -inverse_square, F32)
    q2 = (proj2 * (1.0 / F)).astype(BF16)
    next(summing)

    def second_base(i, carry):
        cols = pl.ds(aligned(i, CHUNK), CHUNK)
        base[:, cols] = u1[:, cols] + jnp.dot(q2, wcat[0:B, cols], preferred_element_type=F32)
        return carry

    lax.fori_loop(0, PIECE // CHUNK, second_base, 0)
    n1 = next(summing)
    spread = F / (n1 + EPS)

    for first in (0, HALF):
        size = first + HALF
        c2[first:size, 0:size] = (m2[first:size, 0:size] * spread[:, 0:size]).astype(BF16)

    def second(i, totals):
        cols = pl.ds(aligned(i, CHUNK), CHUNK)
        out = []
        for first, total in zip((0, HALF), totals):
            size = first + HALF
            value = base[first:size, cols] + jnp.dot(
                c2[first:size, 0:size], u1b[0:size, cols], preferred_element_type=F32
            )
            u2b[first:size, cols] = value.astype(BF16)
            out.append(total + squares_of(value))
        return tuple(out)

    def send_updates(begin, width, stage):
        for d in (1, 7, 4, 2, 6, 3, 5):
            peer = lax.rem(z + d, N)
            send(
                u2b.at[pl.ds(aligned(peer, OWN), OWN), pl.ds(begin, width)],
                u_ref.at[:, pl.ds(aligned(z, PIECE) + begin, width)],
                stage,
                along_z(d),
            )

    squares = second(0, (jnp.zeros((HALF, B), F32),) * 2)
    send_updates(0, CHUNK, 10)
    squares = lax.fori_loop(1, PIECE // CHUNK, second, squares, unroll=True)
    summing = all_sum(as_row(jnp.concatenate(squares, axis=0)), (n2_a, n2_b), 11)
    next(summing)
    send_updates(CHUNK, PIECE - CHUNK, 13)
    keep = pltpu.make_async_copy(u2b.at[own_rows, :], u_ref.at[:, own_cols], load_sem.at[4])
    keep.start()
    next(summing)
    n2 = next(summing)
    scale = jnp.sqrt(F / (n2 + EPS * (n1 + EPS) / F))
    columns[...] = jnp.transpose(jnp.broadcast_to(scale, (B, K)))
    scale_ref[...] = columns[own_rows, :]

    wait_send(near, 0)
    wait_send(early, 14)
    wait_send(late, 15)
    for buf, stage in (
        (proj_xc, 1), (gram_xc, 2), (proj_y, 3), (gram_y, 4), (by_z, 5), (gram, 6), (by_xc, 7),
        (n1_a, 8), (n1_b, 9), (n2_a, 11), (n2_b, 12),
    ):
        wait_send(buf.at[pl.ds(1, buf.shape[0] - 1)], stage)
    keep.wait()
    for begin, width, stage in ((0, CHUNK, 10), (CHUNK, PIECE - CHUNK, 13)):
        sent = u2b.at[pl.ds(0, K - OWN), pl.ds(begin, width)]
        wait_recv(sent, stage)
        wait_send(sent, stage)


def on_device(slab, players):
    def vmem(*shape, dtype=F32):
        return pltpu.VMEM(shape, dtype)

    update, scale = pl.pallas_call(
        kernel,
        out_shape=[
            jax.ShapeDtypeStruct((OWN, LOCAL), BF16),
            jax.ShapeDtypeStruct((OWN, B), F32),
        ],
        in_specs=[pl.BlockSpec(memory_space=pltpu.HBM)] * 2,
        out_specs=[
            pl.BlockSpec(memory_space=pl.ANY),
            pl.BlockSpec(memory_space=pltpu.VMEM),
        ],
        scratch_shapes=[
            vmem(OWN, LOCAL, dtype=BF16),
            vmem(B, LOCAL, dtype=BF16),
            vmem(B + K, PIECE, dtype=BF16),
            vmem(N, 8, B),
            vmem(N, 8, B),
            vmem(N, 8, B),
            vmem(N, 8, B),
            vmem(N, N, 8, B),
            vmem(N, 16, B),
            vmem(N, 16, B),
            vmem(N, 16, B),
            vmem(N, 16, B),
            vmem(B + K, B),
            vmem(K, B + K, dtype=BF16),
            vmem(K, K),
            vmem(K, K, dtype=BF16),
            vmem(K, PIECE),
            vmem(K, PIECE, dtype=BF16),
            vmem(K, PIECE),
            vmem(K, PIECE, dtype=BF16),
            vmem(16, 1, K),
            vmem(32, 1, K),
            vmem(16, 1, K),
            vmem(32, 1, K),
            vmem(K, B),
            pltpu.SemaphoreType.DMA((5,)),
            pltpu.SemaphoreType.DMA((16,)),
            pltpu.SemaphoreType.DMA((16,)),
        ],
        compiler_params=pltpu.CompilerParams(
            collective_id=0, has_side_effects=True, vmem_limit_bytes=52 * 1024 * 1024
        ),
    )(players, slab)
    return (update.astype(F32) * scale[:, 0:1]).astype(BF16)


def solution(mesh):
    split = Mesh(mesh.devices.reshape(N, 8, 4, 2), AXES)
    in_specs = (P(None, FEAT), P("player", FEAT))
    out_specs = P("player", FEAT)
    return jax.shard_map(on_device, mesh=split, in_specs=in_specs, out_specs=out_specs, check_vma=False)
```

```python
import jax
import jax.numpy as jnp
from jax import lax
from jax.experimental import pallas as pl
from jax.experimental.pallas import tpu as pltpu
from jax.sharding import Mesh
from jax.sharding import PartitionSpec as P

F = 524288
EPS = 1e-06
K = 512
B = 128
OWN = 64
LOCAL = 8192
PIECE = 1024
CHUNK = 256
EARLY = 512
N = 8
AXES = ("player", "feat_0", "feat_1", "feat_2")
FEAT = AXES[1:]
MESH = pl.DeviceIdType.MESH
HALF = K // 2
NEAR = (4, 2, 6)
FAR = (3, 5, 1, 7)
F32 = jnp.float32
BF16 = jnp.bfloat16


def aligned(index, unit):
    return pl.multiple_of(index * unit, unit)


def halves_of(value):
    high = value.astype(BF16)
    return high, (value - high.astype(F32)).astype(BF16)


def lower_products(value, out, offset, scale, dtype):
    high, low = halves_of(value)
    left = jnp.concatenate([high, high, low], axis=1)
    right = jnp.concatenate([high, low, high], axis=1)
    for first in (0, HALF):
        size = first + HALF
        corr = lax.dot_general(
            left[first:size], right[0:size], (((1,), (1,)), ((), ())), preferred_element_type=F32
        )
        row = first + lax.broadcasted_iota(jnp.int32, corr.shape, 0)
        earlier = lax.broadcasted_iota(jnp.int32, corr.shape, 1) < row
        out[first:size, offset : offset + size] = jnp.where(earlier, corr * scale, 0.0).astype(dtype)


def kernel(
    w_ref, x_ref, u_ref, scale_ref,
    wv, xv, wcat, proj_part, proj_xc, proj_y, by_z, by_xc, gram_part, gram_xc, gram_y, gram, pg, a1, m2, c2, u1, u1b, base, u2b,
    n1_a, n1_b, n2_a, n2_b, columns,
    load_sem, send_sem, recv_sem,
):
    z = lax.axis_index("player")
    y = lax.axis_index("feat_0")
    x = lax.axis_index("feat_1")
    c = lax.axis_index("feat_2")

    def along_z(d):
        return {"player": lax.rem(z + d, N)}

    def along_y(d):
        return {"feat_0": lax.rem(y + d, N)}

    def along_xc(d):
        return {"feat_1": lax.rem(x + d // 2, 4), "feat_2": lax.rem(c + d % 2, 2)}

    def along_zc(d):
        return {"player": lax.rem(z + d // 2, N), "feat_2": lax.rem(c + d % 2, 2)}

    def along_yx(d):
        return {"feat_0": lax.rem(y + d // 4, N), "feat_1": lax.rem(x + d % 4, 4)}

    def send(src, dst, stage, device):
        pltpu.make_async_remote_copy(
            src_ref=src,
            dst_ref=dst,
            send_sem=send_sem.at[stage],
            recv_sem=recv_sem.at[stage],
            device_id=device,
            device_id_type=MESH,
        ).start()

    def wait_recv(view, stage):
        pltpu.make_async_copy(view, view, recv_sem.at[stage]).wait()

    def wait_send(view, stage):
        pltpu.make_async_copy(view, view, send_sem.at[stage]).wait()

    own_cols = pl.ds(aligned(z, PIECE), PIECE)
    own_rows = pl.ds(aligned(z, OWN), OWN)
    own_in_cat = pl.ds(aligned(z, OWN) + B, OWN)
    load_w = pltpu.make_async_copy(w_ref, wv, load_sem.at[0])
    load_x = pltpu.make_async_copy(x_ref, xv, load_sem.at[1])
    load_own = pltpu.make_async_copy(w_ref.at[:, own_cols], wcat.at[own_in_cat, :], load_sem.at[2])
    load_slab = pltpu.make_async_copy(x_ref.at[:, own_cols], wcat.at[pl.ds(0, B), :], load_sem.at[3])
    load_w.start()
    load_x.start()
    load_own.start()
    load_slab.start()
    barrier = pltpu.get_barrier_semaphore()
    for route, offsets in ((along_zc, range(1, 16)), (along_yx, range(1, 32)), (along_xc, (3, 5, 7))):
        for d in offsets:
            pl.semaphore_signal(barrier, inc=1, device_id=route(d), device_id_type=MESH)
    pl.semaphore_wait(barrier, 49)

    def send_players(offsets, begin, width, stage):
        for d in offsets:
            peer = lax.rem(z + d, N)
            send(
                w_ref.at[:, pl.ds(aligned(peer, PIECE) + begin, width)],
                wcat.at[own_in_cat, pl.ds(begin, width)],
                stage,
                along_z(d),
            )

    send_players(NEAR, 0, PIECE, 0)

    own = 2 * x + c

    def piece_of(d):
        return 2 * lax.rem(x + d // 2, 4) + lax.rem(c + d % 2, 2)

    def rows_times_slab(value):
        return lax.dot_general(value, xv[...], (((1,), (1,)), ((), ())), preferred_element_type=F32)

    def added(first, buf):
        for d in range(1, N):
            first += buf[d]
        return first

    load_w.wait()
    load_x.wait()
    proj_part[...] = rows_times_slab(wv[...]).reshape(N, 8, B)
    for d in range(1, N):
        send(proj_part.at[piece_of(d)], proj_xc.at[d], 1, along_xc(d))
    gram_part[...] = rows_times_slab(xv[...]).reshape(N, 16, B)
    for d in range(1, N):
        send(gram_part.at[piece_of(d)], gram_xc.at[d], 2, along_xc(d))
    wait_recv(proj_xc.at[pl.ds(1, N - 1)], 1)
    proj_y[0] = added(proj_part[own], proj_xc)
    for d in range(1, N):
        send(proj_y.at[0], proj_y.at[d], 3, along_y(d))
    wait_recv(gram_xc.at[pl.ds(1, N - 1)], 2)
    gram_y[0] = added(gram_part[own], gram_xc)
    for d in range(1, N):
        send(gram_y.at[0], gram_y.at[d], 4, along_y(d))
    wait_recv(proj_y.at[pl.ds(1, N - 1)], 3)
    by_z[z] = added(proj_y[0], proj_y)
    for d in range(1, N):
        send(by_z.at[z], by_z.at[z], 5, along_z(d))
    send_players(FAR, 0, EARLY, 14)
    send_players(FAR, EARLY, PIECE - EARLY, 15)
    wait_recv(gram_y.at[pl.ds(1, N - 1)], 4)
    gram[own] = added(gram_y[0], gram_y)
    for d in range(1, N):
        send(gram.at[own], gram.at[own], 6, along_xc(d))
    wait_recv(by_z.at[pl.ds(1, N - 1)], 5)
    by_xc[own] = by_z[...]
    for d in range(1, N):
        send(by_z, by_xc.at[own], 7, along_xc(d))
    wait_recv(by_xc.at[pl.ds(1, N - 1)], 7)
    for i in range(N):
        for j in range(N):
            pg[B + 64 * i + 8 * j : B + 64 * i + 8 * j + 8] = by_xc[j, i]

    inverse_square = 1.0 / F / F
    proj = pg[B : B + K]
    lower_products(proj, a1, B, -inverse_square, BF16)
    a1[:, 0:B] = (proj * (1.0 / F)).astype(BF16)

    load_own.wait()
    load_slab.wait()

    def squares_of(value):
        wide = value * value
        return sum(wide[:, B * i : B * i + B] for i in range(CHUNK // B))

    def as_row(squares):
        return jnp.sum(jnp.transpose(squares), axis=0, keepdims=True)

    near = wcat.at[pl.ds(0, OWN * len(NEAR))]
    early = wcat.at[pl.ds(0, OWN * len(FAR)), pl.ds(0, EARLY)]
    late = wcat.at[pl.ds(0, OWN * len(FAR)), pl.ds(EARLY, PIECE - EARLY)]

    def first_update(i, totals):
        cols = pl.ds(aligned(i, CHUNK), CHUNK)
        out = []
        for first, total in zip((0, HALF), totals):
            size = first + HALF
            value = wcat[B + first : B + size, cols].astype(F32) + jnp.dot(
                a1[first:size, 0 : B + size], wcat[0 : B + size, cols], preferred_element_type=F32
            )
            u1[first:size, cols] = value
            u1b[first:size, cols] = value.astype(BF16)
            out.append(total + squares_of(value))
        return tuple(out)

    wait_recv(near, 0)
    wait_recv(early, 14)
    squares = (jnp.zeros((HALF, B), F32),) * 2
    squares = lax.fori_loop(0, EARLY // CHUNK, first_update, squares, unroll=True)
    wait_recv(late, 15)
    squares = lax.fori_loop(EARLY // CHUNK, PIECE // CHUNK, first_update, squares, unroll=True)

    def hops(d, inner):
        far, near = d // inner, d % inner
        return min(far, N - far) + min(near, inner - near)

    def all_sum(value, bufs, stage):
        for buf, route, inner, s in zip(bufs, (along_zc, along_yx), (2, 4), (stage, stage + 1)):
            count = buf.shape[0]
            buf[0] = value
            for d in sorted(range(1, count), key=lambda d: -hops(d, inner)):
                send(buf.at[0], buf.at[d], s, route(d))
            yield None
            wait_recv(buf.at[pl.ds(1, count - 1)], s)
            for d in range(1, count):
                value += buf[d]
        yield value

    summing = all_sum(as_row(jnp.concatenate(squares, axis=0)), (n1_a, n1_b), 8)
    next(summing)

    wait_recv(gram.at[pl.ds(1, N - 1)], 6)
    for i in range(N):
        pg[16 * i : 16 * i + 16] = gram[i]
    high, low = halves_of(pg[...])
    split = jnp.concatenate([high, low], axis=1)
    proj2 = []
    for first in (0, HALF):
        size = first + HALF
        terms = jnp.dot(a1[first:size, 0 : B + size], split[0 : B + size], preferred_element_type=F32)
        proj2.append(proj[first:size] + terms[:, 0:B] + terms[:, B : 2 * B])
    proj2 = jnp.concatenate(proj2, axis=0)
    lower_products(proj2, m2, 0, -inverse_square, F32)
    q2 = (proj2 * (1.0 / F)).astype(BF16)
    next(summing)

    def second_base(i, carry):
        cols = pl.ds(aligned(i, CHUNK), CHUNK)
        base[:, cols] = u1[:, cols] + jnp.dot(q2, wcat[0:B, cols], preferred_element_type=F32)
        return carry

    lax.fori_loop(0, PIECE // CHUNK, second_base, 0)
    n1 = next(summing)
    spread = F / (n1 + EPS)

    for first in (0, HALF):
        size = first + HALF
        c2[first:size, 0:size] = (m2[first:size, 0:size] * spread[:, 0:size]).astype(BF16)

    def second(i, totals):
        cols = pl.ds(aligned(i, CHUNK), CHUNK)
        out = []
        for first, total in zip((0, HALF), totals):
            size = first + HALF
            value = base[first:size, cols] + jnp.dot(
                c2[first:size, 0:size], u1b[0:size, cols], preferred_element_type=F32
            )
            u2b[first:size, cols] = value.astype(BF16)
            out.append(total + squares_of(value))
        return tuple(out)

    def send_updates(begin, width, stage):
        for d in (1, 7, 2, 6, 3, 5, 4):
            peer = lax.rem(z + d, N)
            send(
                u2b.at[pl.ds(aligned(peer, OWN), OWN), pl.ds(begin, width)],
                u_ref.at[:, pl.ds(aligned(z, PIECE) + begin, width)],
                stage,
                along_z(d),
            )

    squares = second(0, (jnp.zeros((HALF, B), F32),) * 2)
    send_updates(0, CHUNK, 10)
    squares = lax.fori_loop(1, PIECE // CHUNK, second, squares, unroll=True)
    summing = all_sum(as_row(jnp.concatenate(squares, axis=0)), (n2_a, n2_b), 11)
    next(summing)
    send_updates(CHUNK, PIECE - CHUNK, 13)
    keep = pltpu.make_async_copy(u2b.at[own_rows, :], u_ref.at[:, own_cols], load_sem.at[4])
    keep.start()
    next(summing)
    n2 = next(summing)
    scale = jnp.sqrt(F / (n2 + EPS * (n1 + EPS) / F))
    columns[...] = jnp.transpose(jnp.broadcast_to(scale, (B, K)))
    scale_ref[...] = columns[own_rows, :]

    wait_send(near, 0)
    wait_send(early, 14)
    wait_send(late, 15)
    for buf, stage in (
        (proj_xc, 1), (gram_xc, 2), (proj_y, 3), (gram_y, 4), (by_z, 5), (gram, 6), (by_xc, 7),
        (n1_a, 8), (n1_b, 9), (n2_a, 11), (n2_b, 12),
    ):
        wait_send(buf.at[pl.ds(1, buf.shape[0] - 1)], stage)
    keep.wait()
    for begin, width, stage in ((0, CHUNK, 10), (CHUNK, PIECE - CHUNK, 13)):
        sent = u2b.at[pl.ds(0, K - OWN), pl.ds(begin, width)]
        wait_recv(sent, stage)
        wait_send(sent, stage)


def on_device(slab, players):
    def vmem(*shape, dtype=F32):
        return pltpu.VMEM(shape, dtype)

    update, scale = pl.pallas_call(
        kernel,
        out_shape=[
            jax.ShapeDtypeStruct((OWN, LOCAL), BF16),
            jax.ShapeDtypeStruct((OWN, B), F32),
        ],
        in_specs=[pl.BlockSpec(memory_space=pltpu.HBM)] * 2,
        out_specs=[
            pl.BlockSpec(memory_space=pl.ANY),
            pl.BlockSpec(memory_space=pltpu.VMEM),
        ],
        scratch_shapes=[
            vmem(OWN, LOCAL, dtype=BF16),
            vmem(B, LOCAL, dtype=BF16),
            vmem(B + K, PIECE, dtype=BF16),
            vmem(N, 8, B),
            vmem(N, 8, B),
            vmem(N, 8, B),
            vmem(N, 8, B),
            vmem(N, N, 8, B),
            vmem(N, 16, B),
            vmem(N, 16, B),
            vmem(N, 16, B),
            vmem(N, 16, B),
            vmem(B + K, B),
            vmem(K, B + K, dtype=BF16),
            vmem(K, K),
            vmem(K, K, dtype=BF16),
            vmem(K, PIECE),
            vmem(K, PIECE, dtype=BF16),
            vmem(K, PIECE),
            vmem(K, PIECE, dtype=BF16),
            vmem(16, 1, K),
            vmem(32, 1, K),
            vmem(16, 1, K),
            vmem(32, 1, K),
            vmem(K, B),
            pltpu.SemaphoreType.DMA((5,)),
            pltpu.SemaphoreType.DMA((16,)),
            pltpu.SemaphoreType.DMA((16,)),
        ],
        compiler_params=pltpu.CompilerParams(
            collective_id=0, has_side_effects=True, vmem_limit_bytes=52 * 1024 * 1024
        ),
    )(players, slab)
    return (update.astype(F32) * scale[:, 0:1]).astype(BF16)


def solution(mesh):
    split = Mesh(mesh.devices.reshape(N, 8, 4, 2), AXES)
    in_specs = (P(None, FEAT), P("player", FEAT))
    out_specs = P("player", FEAT)
    return jax.shard_map(on_device, mesh=split, in_specs=in_specs, out_specs=out_specs, check_vma=False)
```
